512 devices in a mesh: tm: 64 (over z, x_hi, core), groups: 8 (over y, x_lo).
Axes of the slice: x: 4 (x_hi: 2, x_lo: 2; x = x_hi * 2 + x_lo), y: 4, z: 16, core: 2. Of those that a mesh axis runs over, the one named last changes fastest.
Arguments:
- queries: bfloat16 [65536, 256], P(('groups', 'tm')), parts along dimension 0, may hold values from -6 to 6
- keys: bfloat16 [65536, 256], P(('groups', 'tm')), parts along dimension 0, may hold values from -6 to 6
- values: bfloat16 [65536, 256], P(('groups', 'tm')), parts along dimension 0, may hold values from -6 to 6
- out_grad: bfloat16 [65536, 256], P(('groups', 'tm')), parts along dimension 0, may hold values from -6 to 6
- key_blocks: int32 [512, 6], P(('groups', 'tm')), parts along dimension 0, may hold values from -1 to 63, as said below
Outputs:
- query_grad: bfloat16 [65536, 256], P(('groups', 'tm')), parts along dimension 0
- key_grad: bfloat16 [65536, 256], P(('groups', 'tm')), parts along dimension 0
- value_grad: bfloat16 [65536, 256], P(('groups', 'tm')), parts along dimension 0
The draws below stay inside these ranges and needn't reach their ends.
There are 8 independent parts, one for each index of `groups`. The reference program is written for one: setup_inputs(seed, part) draws one part's arguments, and reference() takes and returns one part's arrays. A program takes and returns all parts, laid end to end along the dimension named above; each array names one. Nothing has to cross between parts.
Inputs may be any that keep to these rules, and one draw needn't show every extreme that they name: `key_blocks`: slot d of row i holds either (i - d) mod 64 or -1; slots 0 to 3 are never -1; some row has no -1, and some row has -1 in every slot from 4 on.
All inputs are finite; a program needn't handle non-finite values.
Results may differ from the reference program's by a relative error of at most 0.033.
Values may be sent and summed in bfloat16 or wider, within the bound.
No kernel may reach another device: no remote copies, remote signals or barrier semaphores. Data moves between devices by JAX's collectives and lax.ppermute only.
A program may use at most 64 MiB of HBM per device.

```python
import jax
import jax.numpy as jnp
from jax import lax

HEAD = 64
D = 256
WIN = 4
REACH = 6
NB = 64
SEQ = 8192


def draw_queries(key, part):
    key = jax.random.fold_in(key, 11)
    base_draw = jax.random.truncated_normal(key, -6.0, 6.0, (SEQ, D), jnp.float32)
    return base_draw.astype(jnp.bfloat16)


def draw_keys(key, part):
    key = jax.random.fold_in(key, 12)
    base_draw = jax.random.truncated_normal(key, -6.0, 6.0, (SEQ, D), jnp.float32)
    return base_draw.astype(jnp.bfloat16)


def draw_key_blocks(key, part):
    key = jax.random.fold_in(key, 13)
    rate_key, choose_key, full_key = jax.random.split(key, 3)
    blocks = jnp.arange(NB, dtype=jnp.int32)
    distances = jnp.arange(REACH, dtype=jnp.int32)
    rates = jax.random.randint(rate_key, (NB, 1), 0, 4)
    rolls = jax.random.randint(choose_key, (NB, REACH), 0, 3)
    include = rolls < rates
    full_row = jax.random.randint(full_key, (), 0, NB)
    empty_row = (full_row + 1) % NB
    include = include | (blocks[:, None] == full_row)
    include = include & (blocks[:, None] != empty_row)
    include = include | (distances[None, :] < WIN)
    sources = (blocks[:, None] - distances[None, :]) % NB
    return jnp.where(include, sources, -1).astype(jnp.int32)


def levels(rng, dims, shards, smallest, high):
    loudness = 1.0
    for dim, parts in shards:
        steps = jax.random.uniform(jax.random.fold_in(jax.random.fold_in(rng, 6), dim), (parts,), jnp.float32, smallest / len(shards), high / len(shards))
        loudness = loudness * jnp.repeat(jnp.exp(steps), dims[dim] // parts).reshape((-1,) + (1,) * (len(dims) - 1 - dim))
    return loudness


def centred(stream_key, extent, spread, most, pieces=(), held_as=jnp.bfloat16):
    drawn = spread * jax.random.normal(stream_key, extent, jnp.float32)
    if pieces:
        drawn = drawn * levels(stream_key, extent, pieces, -0.22, 0.18)
    return jnp.clip(drawn, -most, most).astype(held_as)


def setup_inputs(seed: int = 0, part: int = 0) -> dict:
    splits = jax.random.split(jax.random.key(seed), 6)
    part_keys = jax.random.split(jax.random.fold_in(splits[5], part), 6)
    return {
        "queries": draw_queries(jax.random.fold_in(jax.random.fold_in(splits[5], part), 71), part),
        "keys": draw_keys(jax.random.fold_in(jax.random.fold_in(splits[5], part), 71), part),
        "values": centred(part_keys[2], (SEQ, D), 1.0, 6.0, ((0, 64),)),
        "out_grad": centred(part_keys[3], (SEQ, D), 1.0, 6.0, ((0, 64),)),
        "key_blocks": draw_key_blocks(jax.random.fold_in(jax.random.fold_in(splits[5], part), 71), part),
    }


masked_score = -1.0e30


def reference(queries, keys, values, out_grad, key_blocks):
    block_count = key_blocks.shape[0]
    reach_count = key_blocks.shape[1]
    row_count = queries.shape[0] // block_count
    head_count = D // HEAD
    score_scale = 1.0 / (HEAD ** 0.5)
    query_all = queries.reshape(block_count, row_count, head_count, HEAD)
    key_all = keys.reshape(block_count, row_count, head_count, HEAD)
    value_all = values.reshape(block_count, row_count, head_count, HEAD)
    grad_all = out_grad.reshape(block_count, row_count, head_count, HEAD)
    distances = jnp.arange(reach_count, dtype=jnp.int32)
    causal_keep = jnp.arange(row_count)[None, :] <= jnp.arange(row_count)[:, None]

    def step(carried, query_block):
        key_sum, value_sum = carried
        block_list = key_blocks[query_block]
        sources = ((query_block - distances) % block_count).astype(jnp.int32)
        key_panel = key_all[sources].astype(jnp.float32)
        value_panel = value_all[sources].astype(jnp.float32)
        query_rows = query_all[query_block].astype(jnp.float32)
        grad_rows = grad_all[query_block].astype(jnp.float32)
        logits = jnp.einsum("qhd,rkhd->hqrk", query_rows, key_panel) * score_scale
        allowed = jnp.where((distances == 0)[None, :, None], causal_keep[:, None, :], (block_list >= 0)[None, :, None])
        logits = jnp.where(allowed[None], logits, masked_score)
        peak = jnp.max(logits, axis=(2, 3), keepdims=True)
        log_total = peak + jnp.log(jnp.sum(jnp.exp(logits - peak), axis=(2, 3), keepdims=True))
        weights = jnp.exp(logits - log_total).astype(jnp.bfloat16).astype(jnp.float32)
        output = jnp.einsum("hqrk,rkhd->qhd", weights, value_panel).astype(jnp.bfloat16).astype(jnp.float32)
        row_delta = jnp.sum(grad_rows * output, axis=2).T[:, :, None, None]
        prob_grad = jnp.einsum("qhd,rkhd->hqrk", grad_rows, value_panel)
        score_grad = (weights * (prob_grad - row_delta) * score_scale).astype(jnp.bfloat16).astype(jnp.float32)
        query_part = jnp.einsum("hqrk,rkhd->qhd", score_grad, key_panel)
        key_part = jnp.einsum("hqrk,qhd->rkhd", score_grad, query_rows)
        value_part = jnp.einsum("hqrk,qhd->rkhd", weights, grad_rows)
        key_sum = key_sum.at[sources].add(key_part)
        value_sum = value_sum.at[sources].add(value_part)
        return (key_sum, value_sum), query_part.astype(jnp.bfloat16)

    start = jnp.zeros((block_count, row_count, head_count, HEAD), jnp.float32)
    (key_sum, value_sum), query_parts = lax.scan(step, (start, start), jnp.arange(block_count, dtype=jnp.int32))
    total_rows = block_count * row_count
    return (query_parts.reshape(total_rows, D), key_sum.reshape(total_rows, D).astype(jnp.bfloat16), value_sum.reshape(total_rows, D).astype(jnp.bfloat16))
```

```python
import math

import jax
import jax.numpy as jnp
from jax import lax
from jax.experimental import pallas as pl
from jax.experimental.pallas import tpu as pltpu
from jax.sharding import PartitionSpec as P

HEAD = 64
ROWS = 128
HALF = 128
REACH = 6
FLAGS = 16
MESSAGE = 4 * ROWS + FLAGS
MASKED = -1e30

VMEM = pl.BlockSpec(memory_space=pltpu.VMEM)
SMEM = pl.BlockSpec(memory_space=pltpu.SMEM)


def pack_kernel(blocks_ref, q_ref, k_ref, v_ref, g_ref, out_ref):
    out_ref[0:ROWS, :] = k_ref[...]
    out_ref[ROWS : 2 * ROWS, :] = v_ref[...]
    out_ref[2 * ROWS : 3 * ROWS, :] = q_ref[...]
    out_ref[3 * ROWS : 4 * ROWS, :] = g_ref[...]
    row = lax.broadcasted_iota(jnp.int32, (FLAGS, 2 * HALF), 0)
    flags = jnp.zeros((FLAGS, 2 * HALF), jnp.float32)
    for distance in range(REACH):
        live = (blocks_ref[0, distance] >= 0).astype(jnp.float32)
        flags = jnp.where(row == distance, live, flags)
    out_ref[4 * ROWS :, :] = flags.astype(jnp.bfloat16)


def by_head(rows):
    lane = lax.broadcasted_iota(jnp.int32, rows.shape, 1)
    zero = jnp.zeros_like(rows)
    return jnp.concatenate(
        [jnp.where(lane < HEAD, rows, zero), jnp.where(lane >= HEAD, rows, zero)], axis=0
    )


def grad_kernel(
    core_ref, pair_ref, ahead_ref, behind_ref, far_ref, ahead_got, behind_got, far_got,
    out_ref, keys, values, queries, grads, flags,
):
    core = core_ref[0]

    def put_key(slot, source, start, columns):
        rows = slice(slot * ROWS, (slot + 1) * ROWS)
        keys[rows, :] = source[start : start + ROWS, columns]
        values[rows, :] = source[start + ROWS : start + 2 * ROWS, columns]

    def put_query(slot, source, start, columns):
        rows = slice(slot * ROWS, (slot + 1) * ROWS)
        queries[rows, :] = source[start + 2 * ROWS : start + 3 * ROWS, columns]
        grads[rows, :] = source[start + 3 * ROWS : start + 4 * ROWS, columns]
        flags[slot * FLAGS : (slot + 1) * FLAGS, :] = source[
            start + 4 * ROWS : start + MESSAGE, columns
        ]

    for mine in range(2):

        @pl.when(core == mine)
        def _(mine=mine):
            own = slice(mine * HALF, (mine + 1) * HALF)
            every = slice(0, HALF)
            if mine == 0:
                next1, prev1, on3 = (ahead_ref, own), (behind_ref, own), (far_ref, own)
                next2, prev2, back3 = (ahead_got.at[1], every), (behind_got.at[1], every), (far_got.at[1], every)
            else:
                next1, prev1, on3 = (ahead_got.at[0], every), (behind_got.at[0], every), (far_got.at[0], every)
                next2, prev2, back3 = (ahead_ref, own), (behind_ref, own), (far_ref, own)
            put_key(0, back3[0], 0, back3[1])
            for block in range(2):
                put_key(1 + block, prev2[0], block * 2 * ROWS, prev2[1])
                put_key(3 + block, prev1[0], block * 2 * ROWS, prev1[1])
                put_key(5 + block, pair_ref, block * MESSAGE, own)
                put_key(7 + block, next1[0], block * MESSAGE, next1[1])
                put_key(9 + block, next2[0], block * MESSAGE, next2[1])
                put_query(block, pair_ref, block * MESSAGE, own)
                put_query(2 + block, next1[0], block * MESSAGE, next1[1])
                put_query(4 + block, next2[0], block * MESSAGE, next2[1])
            put_key(11, on3[0], 0, on3[1])
            put_query(6, on3[0], 0, on3[1])

    scale = 1.0 / math.sqrt(HEAD)
    to_base2 = scale * math.log2(math.e)
    both = (((1,), (1,)), ((), ()))
    key_row = lax.broadcasted_iota(jnp.int32, (ROWS, 2 * ROWS), 0)
    query_row = lax.broadcasted_iota(jnp.int32, (ROWS, 2 * ROWS), 1) & (ROWS - 1)
    causal = key_row <= query_row
    lane = lax.broadcasted_iota(jnp.int32, (ROWS, HALF), 1)
    key_grad = [jnp.zeros((ROWS, HALF), jnp.float32) for _ in range(2)]
    value_grad = [jnp.zeros((ROWS, HALF), jnp.float32) for _ in range(2)]

    for slot in range(7):
        rows = slice(slot * ROWS, (slot + 1) * ROWS)
        strip = slice(slot * ROWS, (slot + REACH) * ROWS)
        query_heads = by_head(queries[rows, :])
        grad_heads = by_head(grads[rows, :])
        live = flags[slot * FLAGS : (slot + 1) * FLAGS, :].astype(jnp.float32)
        live = jnp.concatenate([live, live], axis=1)
        strip_keys = keys[strip, :]
        scores = lax.dot_general(strip_keys, query_heads, both, preferred_element_type=jnp.float32)
        prob_grad = lax.dot_general(
            values[strip, :], grad_heads, both, preferred_element_type=jnp.float32
        )
        pieces = [scores[p * ROWS : (p + 1) * ROWS] for p in range(REACH)]
        pieces[0] = jnp.where(live[5:6, :] > 0.0, pieces[0], MASKED)
        pieces[1] = jnp.where(live[4:5, :] > 0.0, pieces[1], MASKED)
        pieces[5] = jnp.where(causal, pieces[5], MASKED)
        grad_pieces = [prob_grad[p * ROWS : (p + 1) * ROWS] for p in range(REACH)]
        peak = pieces[0]
        for piece in pieces[1:]:
            peak = jnp.maximum(peak, piece)
        peak = jnp.max(peak, axis=0, keepdims=True)
        powers = [jnp.exp2((piece - peak) * to_base2) for piece in pieces]
        total = powers[0]
        weighted = powers[0] * grad_pieces[0]
        for power, grad_piece in zip(powers[1:], grad_pieces[1:]):
            total = total + power
            weighted = weighted + power * grad_piece
        inverse = 1.0 / jnp.sum(total, axis=0, keepdims=True)
        row_delta = jnp.sum(weighted, axis=0, keepdims=True) * inverse

        def weights_at(p):
            return (powers[p] * inverse).astype(jnp.bfloat16)

        def score_grad_at(p, weights):
            return (
                weights.astype(jnp.float32) * ((grad_pieces[p] - row_delta) * scale)
            ).astype(jnp.bfloat16)

        needed = range(REACH) if slot < 2 else [p for p in (5 - slot, 6 - slot) if p >= 0]
        weights = {p: weights_at(p) for p in needed}
        score_grads = {p: score_grad_at(p, weights[p]) for p in needed}
        for block in range(2):
            p = 5 + block - slot
            if 0 <= p < REACH:
                key_grad[block] = key_grad[block] + jnp.dot(
                    score_grads[p], query_heads, preferred_element_type=jnp.float32
                )
                value_grad[block] = value_grad[block] + jnp.dot(
                    weights[p], grad_heads, preferred_element_type=jnp.float32
                )
        if slot < 2:
            full = lax.dot_general(
                jnp.concatenate([score_grads[p] for p in range(REACH)], axis=0),
                strip_keys,
                (((0,), (0,)), ((), ())),
                preferred_element_type=jnp.float32,
            )
            query_grad = jnp.where(lane < HEAD, full[:ROWS], full[ROWS:])
            out_ref[slot * 3 * ROWS : (slot * 3 + 1) * ROWS, :] = query_grad.astype(jnp.bfloat16)
    for block in range(2):
        start = block * 3 * ROWS
        out_ref[start + ROWS : start + 2 * ROWS, :] = key_grad[block].astype(jnp.bfloat16)
        out_ref[start + 2 * ROWS : start + 3 * ROWS, :] = value_grad[block].astype(jnp.bfloat16)


def on_device(queries, keys, values, out_grad, key_blocks):
    count = lax.axis_size("tm")
    core = lax.rem(lax.axis_index("tm"), 2)
    cores = [[2 * chip, 2 * chip + 1] for chip in range(count // 2)]

    def send(value, chips_from_core0, chips_from_core1):
        hops = (chips_from_core0, chips_from_core1)
        pairs = [(s, (s + 2 * hops[s % 2]) % count) for s in range(count)]
        return lax.ppermute(value, "tm", pairs)

    def share(value):
        return lax.all_gather(value, "tm", axis_index_groups=cores)

    def swap_halves(value):
        return share(jnp.where(core == 0, value[:, HALF:], value[:, :HALF]))

    own = pl.pallas_call(
        pack_kernel,
        out_shape=jax.ShapeDtypeStruct((MESSAGE, 2 * HALF), jnp.bfloat16),
        in_specs=[SMEM] + [VMEM] * 4,
        out_specs=VMEM,
    )(key_blocks, queries, keys, values, out_grad)
    far = send(own, -3, 3)
    pair = share(own)
    ahead = send(pair.reshape(2 * MESSAGE, 2 * HALF), -1, -2)
    behind = send(pair[:, : 2 * ROWS].reshape(4 * ROWS, 2 * HALF), 1, 2)
    got = swap_halves(jnp.concatenate([behind, far], axis=0))
    behind_got, far_got = got[:, : 4 * ROWS], got[:, 4 * ROWS :]
    ahead_got = swap_halves(ahead)
    result = pl.pallas_call(
        grad_kernel,
        out_shape=jax.ShapeDtypeStruct((6 * ROWS, HALF), jnp.bfloat16),
        in_specs=[SMEM] + [VMEM] * 7,
        out_specs=VMEM,
        scratch_shapes=[
            pltpu.VMEM((12 * ROWS, HALF), jnp.bfloat16),
            pltpu.VMEM((12 * ROWS, HALF), jnp.bfloat16),
            pltpu.VMEM((7 * ROWS, HALF), jnp.bfloat16),
            pltpu.VMEM((7 * ROWS, HALF), jnp.bfloat16),
            pltpu.VMEM((7 * FLAGS, HALF), jnp.bfloat16),
        ],
        compiler_params=pltpu.CompilerParams(vmem_limit_bytes=24 * 1024 * 1024),
    )(
        core.reshape(1), pair.reshape(2 * MESSAGE, 2 * HALF), ahead, behind, far,
        ahead_got, behind_got, far_got,
    )
    both = share(result)
    mine = lax.dynamic_slice(both, (0, core * 3 * ROWS, 0), (2, 3 * ROWS, HALF))
    mine = jnp.concatenate([mine[0], mine[1]], axis=1)
    return mine[:ROWS], mine[ROWS : 2 * ROWS], mine[2 * ROWS :]


def solution(mesh):
    rows = P(("groups", "tm"), None)
    return jax.shard_map(
        on_device,
        mesh=mesh,
        in_specs=(rows,) * 5,
        out_specs=(rows,) * 3,
        check_vma=False,
    )
```

```python
import math

import jax
import jax.numpy as jnp
from jax import lax
from jax.experimental import pallas as pl
from jax.experimental.pallas import tpu as pltpu
from jax.sharding import PartitionSpec as P

HEAD = 64
ROWS = 128
HALF = 128
REACH = 6
FLAGS = 16
MESSAGE = 4 * ROWS + FLAGS
MASKED = -1e30
GRANT = 16 * 1024 * 1024

VMEM = pl.BlockSpec(memory_space=pltpu.VMEM)
SMEM = pl.BlockSpec(memory_space=pltpu.SMEM)


def pack_kernel(blocks_ref, q_ref, k_ref, v_ref, g_ref, out_ref, pair_ref):
    for ref, start in ((k_ref, 0), (v_ref, ROWS)):
        rows = ref[...]
        out_ref[start : start + ROWS, :] = rows
        pair_ref[start : start + ROWS, :] = rows
    out_ref[2 * ROWS : 3 * ROWS, :] = q_ref[...]
    out_ref[3 * ROWS : 4 * ROWS, :] = g_ref[...]
    row = lax.broadcasted_iota(jnp.int32, (FLAGS, 2 * HALF), 0)
    flags = jnp.zeros((FLAGS, 2 * HALF), jnp.float32)
    for distance in range(REACH):
        live = (blocks_ref[0, distance] >= 0).astype(jnp.float32)
        flags = jnp.where(row == distance, live, flags)
    out_ref[4 * ROWS :, :] = flags.astype(jnp.bfloat16)


def by_head(rows):
    lane = lax.broadcasted_iota(jnp.int32, rows.shape, 1)
    zero = jnp.zeros_like(rows)
    return jnp.concatenate(
        [jnp.where(lane < HEAD, rows, zero), jnp.where(lane >= HEAD, rows, zero)], axis=0
    )


def take(source, start, count, columns, target, at):
    target[at * ROWS : (at + count) * ROWS, :] = source[start : start + count * ROWS, columns]


def on_core(core, place):
    own = (slice(0, HALF), slice(HALF, 2 * HALF))
    for mine in range(2):

        @pl.when(core == mine)
        def _(mine=mine):
            place(mine, own[mine])


def query_step(strip_keys, strip_values, query_rows, grad_rows, live, needed):
    scale = 1.0 / math.sqrt(HEAD)
    to_base2 = scale * math.log2(math.e)
    both = (((1,), (1,)), ((), ()))
    key_row = lax.broadcasted_iota(jnp.int32, (ROWS, 2 * ROWS), 0)
    query_row = lax.broadcasted_iota(jnp.int32, (ROWS, 2 * ROWS), 1) & (ROWS - 1)
    query_heads = by_head(query_rows)
    grad_heads = by_head(grad_rows)
    live = live.astype(jnp.float32)
    live = jnp.concatenate([live, live], axis=1)
    scores = lax.dot_general(strip_keys, query_heads, both, preferred_element_type=jnp.float32)
    prob_grad = lax.dot_general(
        strip_values, grad_heads, both, preferred_element_type=jnp.float32
    )
    pieces = [scores[p * ROWS : (p + 1) * ROWS] for p in range(REACH)]
    pieces[0] = jnp.where(live[5:6, :] > 0.0, pieces[0], MASKED)
    pieces[1] = jnp.where(live[4:5, :] > 0.0, pieces[1], MASKED)
    pieces[5] = jnp.where(key_row <= query_row, pieces[5], MASKED)
    grad_pieces = [prob_grad[p * ROWS : (p + 1) * ROWS] for p in range(REACH)]
    peak = pieces[0]
    for piece in pieces[1:]:
        peak = jnp.maximum(peak, piece)
    peak = jnp.max(peak, axis=0, keepdims=True)
    powers = [jnp.exp2((piece - peak) * to_base2) for piece in pieces]
    total = powers[0]
    weighted = powers[0] * grad_pieces[0]
    for power, grad_piece in zip(powers[1:], grad_pieces[1:]):
        total = total + power
        weighted = weighted + power * grad_piece
    inverse = 1.0 / jnp.sum(total, axis=0, keepdims=True)
    row_delta = jnp.sum(weighted, axis=0, keepdims=True) * inverse
    weights, score_grads = {}, {}
    for p in needed:
        weights[p] = (powers[p] * inverse).astype(jnp.bfloat16)
        score_grads[p] = (
            weights[p].astype(jnp.float32) * ((grad_pieces[p] - row_delta) * scale)
        ).astype(jnp.bfloat16)
    return query_heads, grad_heads, weights, score_grads


def dots(step, p, sums, key):
    query_heads, grad_heads, weights, score_grads = step
    parts = (
        jnp.dot(score_grads[p], query_heads, preferred_element_type=jnp.float32),
        jnp.dot(weights[p], grad_heads, preferred_element_type=jnp.float32),
    )
    sums[key] = parts if key not in sums else tuple(s + part for s, part in zip(sums[key], parts))


def query_part(strip_keys, score_grads):
    full = lax.dot_general(
        jnp.concatenate([score_grads[p] for p in range(REACH)], axis=0),
        strip_keys,
        (((0,), (0,)), ((), ())),
        preferred_element_type=jnp.float32,
    )
    lane = lax.broadcasted_iota(jnp.int32, (ROWS, HALF), 1)
    return jnp.where(lane < HEAD, full[:ROWS], full[ROWS:]).astype(jnp.bfloat16)


def block_of(ref, index):
    start = index * MESSAGE
    parts = [ref[start + i * ROWS : start + (i + 1) * ROWS, :] for i in range(4)]
    return (*parts, ref[start + 4 * ROWS : start + MESSAGE, :])


def write_sums(ref, sums, first):
    for block in range(2):
        for which in range(2):
            start = (2 * block + which) * ROWS
            ref[start : start + ROWS, :] = sums[first + block][which].astype(ref.dtype)


def read_sums(ref, first):
    return {
        first + block: tuple(
            ref[(2 * block + w) * ROWS : (2 * block + w + 1) * ROWS, :].astype(jnp.float32) for w in range(2)
        )
        for block in range(2)
    }


def own_kernel(
    core_ref, own_ref, behind_ref, far_ref, got_ref,
    keys, values, query_grad, own_sums, back_sums,
):
    every = slice(0, HALF)

    def place(mine, own):
        if mine == 0:
            near, next_, last = (behind_ref, own, 0), (got_ref.at[1], every, 0), (got_ref.at[1], every, 4 * ROWS)
        else:
            near, next_, last = (got_ref.at[0], every, 0), (behind_ref, own, 0), (far_ref, own, 0)
        for (ref, columns, start), first, count in ((last, 0, 1), (next_, 1, 2), (near, 3, 2)):
            for block in range(count):
                take(ref, start + block * 2 * ROWS, 1, columns, keys, first + block)
                take(ref, start + block * 2 * ROWS + ROWS, 1, columns, values, first + block)

    on_core(core_ref[0], place)
    blocks = [block_of(own_ref, block) for block in range(2)]
    for block in range(2):
        rows = slice((5 + block) * ROWS, (6 + block) * ROWS)
        keys[rows, :] = blocks[block][0]
        values[rows, :] = blocks[block][1]
    sums = {}
    for slot in range(2):
        strip = slice(slot * ROWS, (slot + REACH) * ROWS)
        strip_keys = keys[strip, :]
        step = query_step(strip_keys, values[strip, :], *blocks[slot][2:], list(range(REACH)))
        for p in range(REACH):
            if slot + p not in (0, 3, 4):
                dots(step, p, sums, slot + p)
        query_grad[slot * ROWS : (slot + 1) * ROWS, :] = query_part(strip_keys, step[3])
    write_sums(own_sums, sums, 5)
    write_sums(back_sums, sums, 1)


def ahead_step(slot, first, ahead_ref, keys, values, needed, sums):
    strip = slice((slot - first) * ROWS, (slot - first + REACH) * ROWS)
    step = query_step(keys[strip, :], values[strip, :], *block_of(ahead_ref, slot - 2)[2:], needed)
    for p in needed:
        dots(step, p, sums, slot + p)


def ahead_kernel(ahead_ref, keys7, values7, own_in, back_in, own_out, back_out, keys, values):
    for target, source, part in ((keys, keys7, 0), (values, values7, 1)):
        target[: 5 * ROWS, :] = source[2 * ROWS :, :]
        target[5 * ROWS :, :] = block_of(ahead_ref, 0)[part]
    sums = read_sums(own_in, 5) | read_sums(back_in, 1)
    ahead_step(2, 2, ahead_ref, keys, values, [0, 3, 4], sums)
    write_sums(own_out, sums, 5)
    write_sums(back_out, sums, 1)


def after_kernel(ahead_ref, keys7, values7, own_in, own_out, keys, values):
    for target, source, part in ((keys, keys7, 0), (values, values7, 1)):
        target[: 4 * ROWS, :] = source[3 * ROWS :, :]
        for block in range(2):
            target[(4 + block) * ROWS : (5 + block) * ROWS, :] = block_of(ahead_ref, block)[part]
    sums = read_sums(own_in, 5)
    ahead_step(3, 3, ahead_ref, keys, values, [2, 3], sums)
    write_sums(own_out, sums, 5)


def total_of(sums_ref, back_ref, block, which):
    rows = slice((2 * block + which) * ROWS, (2 * block + which + 1) * ROWS)
    return (sums_ref[rows, :] + back_ref[rows, :].astype(jnp.float32)).astype(jnp.bfloat16)


def swap_kernel(core_ref, query_grad, sums_ref, back_ref, out_ref):
    def place(mine, own):
        del own
        other = 1 - mine
        out_ref[:ROWS, :] = query_grad[other * ROWS : (other + 1) * ROWS, :]
        for which in range(2):
            out_ref[(1 + which) * ROWS : (2 + which) * ROWS, :] = total_of(sums_ref, back_ref, other, which)

    on_core(core_ref[0], place)


def last_kernel(core_ref, query_grad, sums_ref, back_ref, got_ref, out_q, out_k, out_v):
    def place(mine, own):
        other = slice((1 - mine) * HALF, (2 - mine) * HALF)
        out_q[:, own] = query_grad[mine * ROWS : (mine + 1) * ROWS, :]
        for which, out in ((0, out_k), (1, out_v)):
            out[:, own] = total_of(sums_ref, back_ref, mine, which)
        for at, out in enumerate((out_q, out_k, out_v)):
            out[:, other] = got_ref[1 - mine, at * ROWS : (at + 1) * ROWS, :]

    on_core(core_ref[0], place)


def call(kernel, name, outs, operands, scratch=(), work=0, scalar=True, grant=GRANT):
    outs = [jax.ShapeDtypeStruct(shape, dtype) for shape, dtype in outs]
    return pl.pallas_call(
        kernel,
        name=name,
        out_shape=outs,
        in_specs=[SMEM] * scalar + [VMEM] * (len(operands) - scalar),
        out_specs=[VMEM] * len(outs),
        scratch_shapes=[pltpu.VMEM((rows, HALF), jnp.bfloat16) for rows in scratch],
        cost_estimate=pl.CostEstimate(
            flops=work * 4 * 768 * 128 * 256, bytes_accessed=work * 1_000_000, transcendentals=work * 768 * 256
        ),
        compiler_params=pltpu.CompilerParams(vmem_limit_bytes=grant),
    )(*operands)


def on_device(queries, keys, values, out_grad, key_blocks):
    bf16, f32 = jnp.bfloat16, jnp.float32
    count = lax.axis_size("tm")
    core = lax.rem(lax.axis_index("tm"), 2)
    which = core.reshape(1)
    cores = [[2 * chip, 2 * chip + 1] for chip in range(count // 2)]

    def send(value, chips_from_core0, chips_from_core1):
        hops = (chips_from_core0, chips_from_core1)
        pairs = [(s, (s + 2 * hops[s % 2]) % count) for s in range(count) if hops[s % 2]]
        return lax.ppermute(value, "tm", pairs)

    def share(value):
        return lax.all_gather(value, "tm", axis_index_groups=cores)

    def half(value, other):
        return jnp.where((core == 0) != other, value[:, :HALF], value[:, HALF:])

    own, own_pair = pl.pallas_call(
        pack_kernel,
        name="pack",
        out_shape=[
            jax.ShapeDtypeStruct((MESSAGE, 2 * HALF), bf16),
            jax.ShapeDtypeStruct((2 * ROWS, 2 * HALF), bf16),
        ],
        in_specs=[SMEM] + [VMEM] * 4,
        out_specs=[VMEM] * 2,
    )(key_blocks, queries, keys, values, out_grad)
    far = send(own_pair, 0, 3)
    pair = share(own)
    behind = send(pair[:, : 2 * ROWS].reshape(4 * ROWS, 2 * HALF), 1, 2)
    ours = half(pair.reshape(2 * MESSAGE, 2 * HALF), False)
    ahead = send(ours, -1, -1)
    got = share(half(jnp.concatenate([behind, far], axis=0), True))
    seven, sums_of = ((7 * ROWS, HALF), bf16), (4 * ROWS, HALF)
    keys7, values7, query_grad, sums, back = call(
        own_kernel, "own", [seven, seven, ((2 * ROWS, HALF), bf16), (sums_of, f32), (sums_of, f32)],
        (which, ours, behind, far, got), work=2,
    )
    sums, back = call(
        ahead_kernel, "ahead", [(sums_of, f32), (sums_of, bf16)], (ahead, keys7, values7, sums, back),
        (6 * ROWS, 6 * ROWS), work=1, scalar=False,
    )
    returned = send(back, -2, -2)
    (sums,) = call(
        after_kernel, "after", [(sums_of, f32)], (ahead, keys7, values7, sums), (6 * ROWS, 6 * ROWS),
        work=1, scalar=False,
    )
    (swap,) = call(
        swap_kernel, "swap", [((3 * ROWS, HALF), bf16)], (which, query_grad, sums, returned)
    )
    return tuple(
        call(
            last_kernel, "last", [((ROWS, 2 * HALF), bf16)] * 3,
            (which, query_grad, sums, returned, share(swap)),
        )
    )


def solution(mesh):
    rows = P(("groups", "tm"), None)
    return jax.shard_map(
        on_device,
        mesh=mesh,
        in_specs=(rows,) * 5,
        out_specs=(rows,) * 3,
        check_vma=False,
    )
```

```python
import math

import jax
import jax.numpy as jnp
from jax import lax
from jax.experimental import pallas as pl
from jax.experimental.pallas import tpu as pltpu
from jax.sharding import PartitionSpec as P

HEAD = 64
ROWS = 128
HALF = 128
REACH = 6
FLAGS = 16
MESSAGE = 4 * ROWS + FLAGS
MASKED = -1e30
GRANT = 16 * 1024 * 1024

VMEM = pl.BlockSpec(memory_space=pltpu.VMEM)
SMEM = pl.BlockSpec(memory_space=pltpu.SMEM)


def pack_kernel(blocks_ref, q_ref, k_ref, v_ref, g_ref, out_ref, pair_ref):
    for ref, start in ((k_ref, 0), (v_ref, ROWS)):
        rows = ref[...]
        out_ref[start : start + ROWS, :] = rows
        pair_ref[start : start + ROWS, :] = rows
    out_ref[2 * ROWS : 3 * ROWS, :] = q_ref[...]
    out_ref[3 * ROWS : 4 * ROWS, :] = g_ref[...]
    row = lax.broadcasted_iota(jnp.int32, (FLAGS, 2 * HALF), 0)
    flags = jnp.zeros((FLAGS, 2 * HALF), jnp.float32)
    for distance in range(REACH):
        live = (blocks_ref[0, distance] >= 0).astype(jnp.float32)
        flags = jnp.where(row == distance, live, flags)
    out_ref[4 * ROWS :, :] = flags.astype(jnp.bfloat16)


def by_head(rows):
    lane = lax.broadcasted_iota(jnp.int32, rows.shape, 1)
    zero = jnp.zeros_like(rows)
    return jnp.concatenate(
        [jnp.where(lane < HEAD, rows, zero), jnp.where(lane >= HEAD, rows, zero)], axis=0
    )


def take(source, start, count, columns, target, at):
    target[at * ROWS : (at + count) * ROWS, :] = source[start : start + count * ROWS, columns]


def on_core(core, place):
    own = (slice(0, HALF), slice(HALF, 2 * HALF))
    for mine in range(2):

        @pl.when(core == mine)
        def _(mine=mine):
            place(mine, own[mine])


def query_step(strip_keys, strip_values, query_rows, grad_rows, live, needed):
    scale = 1.0 / math.sqrt(HEAD)
    to_base2 = scale * math.log2(math.e)
    both = (((1,), (1,)), ((), ()))
    key_row = lax.broadcasted_iota(jnp.int32, (ROWS, 2 * ROWS), 0)
    query_row = lax.broadcasted_iota(jnp.int32, (ROWS, 2 * ROWS), 1) & (ROWS - 1)
    query_heads = by_head(query_rows)
    grad_heads = by_head(grad_rows)
    live = live.astype(jnp.float32)
    live = jnp.concatenate([live, live], axis=1)
    scores = lax.dot_general(strip_keys, query_heads, both, preferred_element_type=jnp.float32)
    prob_grad = lax.dot_general(
        strip_values, grad_heads, both, preferred_element_type=jnp.float32
    )
    pieces = [scores[p * ROWS : (p + 1) * ROWS] for p in range(REACH)]
    pieces[0] = jnp.where(live[5:6, :] > 0.0, pieces[0], MASKED)
    pieces[1] = jnp.where(live[4:5, :] > 0.0, pieces[1], MASKED)
    pieces[5] = jnp.where(key_row <= query_row, pieces[5], MASKED)
    grad_pieces = [prob_grad[p * ROWS : (p + 1) * ROWS] for p in range(REACH)]
    peak = pieces[0]
    for piece in pieces[1:]:
        peak = jnp.maximum(peak, piece)
    peak = jnp.max(peak, axis=0, keepdims=True)
    powers = [jnp.exp2((piece - peak) * to_base2) for piece in pieces]
    total = powers[0]
    weighted = powers[0] * grad_pieces[0]
    for power, grad_piece in zip(powers[1:], grad_pieces[1:]):
        total = total + power
        weighted = weighted + power * grad_piece
    inverse = 1.0 / jnp.sum(total, axis=0, keepdims=True)
    row_delta = jnp.sum(weighted, axis=0, keepdims=True) * inverse
    weights, score_grads = {}, {}
    for p in needed:
        weights[p] = (powers[p] * inverse).astype(jnp.bfloat16)
        score_grads[p] = (
            weights[p].astype(jnp.float32) * ((grad_pieces[p] - row_delta) * scale)
        ).astype(jnp.bfloat16)
    return query_heads, grad_heads, weights, score_grads


def dots(step, p, sums, key):
    query_heads, grad_heads, weights, score_grads = step
    parts = (
        jnp.dot(score_grads[p], query_heads, preferred_element_type=jnp.float32),
        jnp.dot(weights[p], grad_heads, preferred_element_type=jnp.float32),
    )
    sums[key] = parts if key not in sums else tuple(s + part for s, part in zip(sums[key], parts))


def query_part(strip_keys, score_grads):
    full = lax.dot_general(
        jnp.concatenate([score_grads[p] for p in range(REACH)], axis=0),
        strip_keys,
        (((0,), (0,)), ((), ())),
        preferred_element_type=jnp.float32,
    )
    lane = lax.broadcasted_iota(jnp.int32, (ROWS, HALF), 1)
    return jnp.where(lane < HEAD, full[:ROWS], full[ROWS:]).astype(jnp.bfloat16)


def block_of(ref, index):
    start = index * MESSAGE
    parts = [ref[start + i * ROWS : start + (i + 1) * ROWS, :] for i in range(4)]
    return (*parts, ref[start + 4 * ROWS : start + MESSAGE, :])


def write_sums(ref, sums, first):
    for block in range(2):
        for which in range(2):
            start = (2 * block + which) * ROWS
            ref[start : start + ROWS, :] = sums[first + block][which].astype(ref.dtype)


def read_sums(ref, first):
    return {
        first + block: tuple(
            ref[(2 * block + w) * ROWS : (2 * block + w + 1) * ROWS, :].astype(jnp.float32) for w in range(2)
        )
        for block in range(2)
    }


def own_kernel(core_ref, own_ref, behind_ref, far_ref, got_ref, keys, values, back_sums):
    every = slice(0, HALF)

    def place(mine, own):
        if mine == 0:
            near, next_, last = (behind_ref, own, 0), (got_ref.at[1], every, 2 * ROWS), (got_ref.at[1], every, 0)
        else:
            near, next_, last = (got_ref.at[0], every, 2 * ROWS), (behind_ref, own, 0), (far_ref, own, 0)
        for (ref, columns, start), first, count in ((last, 0, 1), (next_, 1, 2), (near, 3, 2)):
            for block in range(count):
                take(ref, start + block * 2 * ROWS, 1, columns, keys, first + block)
                take(ref, start + block * 2 * ROWS + ROWS, 1, columns, values, first + block)

    on_core(core_ref[0], place)
    blocks = [block_of(own_ref, block) for block in range(2)]
    for block in range(2):
        rows = slice((5 + block) * ROWS, (6 + block) * ROWS)
        keys[rows, :] = blocks[block][0]
        values[rows, :] = blocks[block][1]
    sums = {}
    for slot in range(2):
        strip_step(slot, 0, blocks[slot], keys, values, [1 - slot, 2 - slot], sums)
    write_sums(back_sums, sums, 1)


def strip_step(slot, first, block, keys, values, needed, sums):
    strip = slice((slot - first) * ROWS, (slot - first + REACH) * ROWS)
    step = query_step(keys[strip, :], values[strip, :], *block[2:], needed)
    for p in needed:
        if slot + p in (1, 2, 5, 6):
            dots(step, p, sums, slot + p)
    return step


def ahead_kernel(ahead_ref, keys7, values7, back_in, back_out, keys, values):
    for target, source, part in ((keys, keys7, 0), (values, values7, 1)):
        target[: 5 * ROWS, :] = source[2 * ROWS :, :]
        target[5 * ROWS :, :] = block_of(ahead_ref, 0)[part]
    sums = read_sums(back_in, 1)
    strip_step(2, 2, block_of(ahead_ref, 0), keys, values, [0], sums)
    write_sums(back_out, sums, 1)


def after_kernel(own_ref, ahead_ref, keys7, values7, query_grad, own_sums, keys, values):
    for target, source, part in ((keys, keys7, 0), (values, values7, 1)):
        target[: 7 * ROWS, :] = source[...]
        for block in range(2):
            target[(7 + block) * ROWS : (8 + block) * ROWS, :] = block_of(ahead_ref, block)[part]
    sums = {}
    for slot in range(4):
        block = block_of((own_ref, ahead_ref)[slot // 2], slot % 2)
        needed = list(range(REACH)) if slot < 2 else [5 - slot, 6 - slot]
        if slot < 2:
            strip = slice(slot * ROWS, (slot + REACH) * ROWS)
            step = query_step(keys[strip, :], values[strip, :], *block[2:], needed)
            for p in range(5 - slot, REACH):
                dots(step, p, sums, slot + p)
            query_grad[slot * ROWS : (slot + 1) * ROWS, :] = query_part(keys[strip, :], step[3])
        else:
            strip_step(slot, 0, block, keys, values, needed, sums)
    write_sums(own_sums, sums, 5)


def pick_kernel(core_ref, value_ref, out_ref):
    def place(mine, own):
        del own
        out_ref[...] = value_ref[:, (1 - mine) * HALF : (2 - mine) * HALF]

    on_core(core_ref[0], place)


def total_of(sums_ref, back_ref, block, which):
    rows = slice((2 * block + which) * ROWS, (2 * block + which + 1) * ROWS)
    return (sums_ref[rows, :] + back_ref[rows, :].astype(jnp.float32)).astype(jnp.bfloat16)


def swap_kernel(core_ref, query_grad, sums_ref, back_ref, out_ref):
    def place(mine, own):
        del own
        other = 1 - mine
        out_ref[:ROWS, :] = query_grad[other * ROWS : (other + 1) * ROWS, :]
        for which in range(2):
            out_ref[(1 + which) * ROWS : (2 + which) * ROWS, :] = total_of(sums_ref, back_ref, other, which)

    on_core(core_ref[0], place)


def last_kernel(core_ref, query_grad, sums_ref, back_ref, got_ref, out_q, out_k, out_v):
    def place(mine, own):
        other = slice((1 - mine) * HALF, (2 - mine) * HALF)
        out_q[:, own] = query_grad[mine * ROWS : (mine + 1) * ROWS, :]
        for which, out in ((0, out_k), (1, out_v)):
            out[:, own] = total_of(sums_ref, back_ref, mine, which)
        for at, out in enumerate((out_q, out_k, out_v)):
            out[:, other] = got_ref[1 - mine, at * ROWS : (at + 1) * ROWS, :]

    on_core(core_ref[0], place)


def call(kernel, name, outs, operands, scratch=(), work=0, scalar=True, grant=GRANT):
    outs = [jax.ShapeDtypeStruct(shape, dtype) for shape, dtype in outs]
    return pl.pallas_call(
        kernel,
        name=name,
        out_shape=outs,
        in_specs=[SMEM] * scalar + [VMEM] * (len(operands) - scalar),
        out_specs=[VMEM] * len(outs),
        scratch_shapes=[pltpu.VMEM((rows, HALF), jnp.bfloat16) for rows in scratch],
        cost_estimate=pl.CostEstimate(
            flops=work * 4 * 768 * 128 * 256, bytes_accessed=work * 1_000_000, transcendentals=work * 768 * 256
        ),
        compiler_params=pltpu.CompilerParams(vmem_limit_bytes=grant),
    )(*operands)


def on_device(queries, keys, values, out_grad, key_blocks):
    bf16, f32 = jnp.bfloat16, jnp.float32
    count = lax.axis_size("tm")
    core = lax.rem(lax.axis_index("tm"), 2)
    which = core.reshape(1)
    cores = [[2 * chip, 2 * chip + 1] for chip in range(count // 2)]

    def send(value, chips_from_core0, chips_from_core1):
        hops = (chips_from_core0, chips_from_core1)
        pairs = [(s, (s + 2 * hops[s % 2]) % count) for s in range(count) if hops[s % 2]]
        return lax.ppermute(value, "tm", pairs)

    def share(value):
        return lax.all_gather(value, "tm", axis_index_groups=cores)

    def half(value, other):
        return jnp.where((core == 0) != other, value[:, :HALF], value[:, HALF:])

    own, own_pair = pl.pallas_call(
        pack_kernel,
        name="pack",
        out_shape=[
            jax.ShapeDtypeStruct((MESSAGE, 2 * HALF), bf16),
            jax.ShapeDtypeStruct((2 * ROWS, 2 * HALF), bf16),
        ],
        in_specs=[SMEM] + [VMEM] * 4,
        out_specs=[VMEM] * 2,
    )(key_blocks, queries, keys, values, out_grad)
    far = send(own_pair, 0, 3)
    pair = share(own)
    behind = send(pair[:, : 2 * ROWS].reshape(4 * ROWS, 2 * HALF), 1, 2)
    ours = half(pair.reshape(2 * MESSAGE, 2 * HALF), False)
    ahead = send(ours, -1, -1)
    (far_half,) = call(pick_kernel, "pick", [((2 * ROWS, HALF), bf16)], (which, far), work=2)
    got = share(jnp.concatenate([far_half, half(behind, True)], axis=0))
    seven, sums_of = ((7 * ROWS, HALF), bf16), (4 * ROWS, HALF)
    keys7, values7, back = call(
        own_kernel, "own", [seven, seven, (sums_of, f32)], (which, ours, behind, far, got), work=2
    )
    (back,) = call(
        ahead_kernel, "ahead", [(sums_of, bf16)], (ahead, keys7, values7, back),
        (6 * ROWS, 6 * ROWS), work=1, scalar=False,
    )
    returned = send(back, -2, -2)
    query_grad, sums = call(
        after_kernel, "after", [((2 * ROWS, HALF), bf16), (sums_of, f32)], (ours, ahead, keys7, values7),
        (9 * ROWS, 9 * ROWS), work=4, scalar=False,
    )
    (swap,) = call(
        swap_kernel, "swap", [((3 * ROWS, HALF), bf16)], (which, query_grad, sums, returned)
    )
    return tuple(
        call(
            last_kernel, "last", [((ROWS, 2 * HALF), bf16)] * 3,
            (which, query_grad, sums, returned, share(swap)),
        )
    )


def solution(mesh):
    rows = P(("groups", "tm"), None)
    return jax.shard_map(
        on_device,
        mesh=mesh,
        in_specs=(rows,) * 5,
        out_specs=(rows,) * 3,
        check_vma=False,
    )
```

```python
import math

import jax
import jax.numpy as jnp
from jax import lax
from jax.experimental import pallas as pl
from jax.experimental.pallas import tpu as pltpu
from jax.sharding import PartitionSpec as P

HEAD = 64
ROWS = 128
HALF = 128
REACH = 6
FLAGS = 16
MESSAGE = 4 * ROWS + FLAGS
MASKED = -1e30
GRANT = 16 * 1024 * 1024

VMEM = pl.BlockSpec(memory_space=pltpu.VMEM)
SMEM = pl.BlockSpec(memory_space=pltpu.SMEM)


def placed(parts, rows, columns):
    total = None
    for part, row, column in parts:
        space = [(row, rows - row - part.shape[0], 0), (column, columns - column - part.shape[1], 0)]
        padded = lax.pad(part, jnp.array(-jnp.inf, part.dtype), space)
        total = padded if total is None else jnp.maximum(total, padded)
    return total


def by_head(rows):
    lane = lax.broadcasted_iota(jnp.int32, rows.shape, 1)
    zero = jnp.zeros_like(rows)
    return jnp.concatenate(
        [jnp.where(lane < HEAD, rows, zero), jnp.where(lane >= HEAD, rows, zero)], axis=0
    )


def take(source, start, count, columns, target, at):
    target[at * ROWS : (at + count) * ROWS, :] = source[start : start + count * ROWS, columns]


def on_core(core, place):
    own = (slice(0, HALF), slice(HALF, 2 * HALF))
    for mine in range(2):

        @pl.when(core == mine)
        def _(mine=mine):
            place(mine, own[mine])


def live_at(live, distance):
    return jnp.broadcast_to(live[:1, distance : distance + 1], (1, 2 * ROWS)) > 0.0


def query_step(strip_keys, strip_values, query_rows, grad_rows, live, needed):
    scale = 1.0 / math.sqrt(HEAD)
    to_base2 = scale * math.log2(math.e)
    both = (((1,), (1,)), ((), ()))
    key_row = lax.broadcasted_iota(jnp.int32, (ROWS, 2 * ROWS), 0)
    query_row = lax.broadcasted_iota(jnp.int32, (ROWS, 2 * ROWS), 1) & (ROWS - 1)
    query_heads = by_head(query_rows)
    grad_heads = by_head(grad_rows)
    live = live.astype(jnp.float32)
    scores = lax.dot_general(strip_keys, query_heads, both, preferred_element_type=jnp.float32)
    prob_grad = lax.dot_general(
        strip_values, grad_heads, both, preferred_element_type=jnp.float32
    )
    pieces = [scores[p * ROWS : (p + 1) * ROWS] for p in range(REACH)]
    pieces[0] = jnp.where(live_at(live, 5), pieces[0], MASKED)
    pieces[1] = jnp.where(live_at(live, 4), pieces[1], MASKED)
    pieces[5] = jnp.where(key_row <= query_row, pieces[5], MASKED)
    grad_pieces = [prob_grad[p * ROWS : (p + 1) * ROWS] for p in range(REACH)]
    peak = pieces[0]
    for piece in pieces[1:]:
        peak = jnp.maximum(peak, piece)
    peak = jnp.max(peak, axis=0, keepdims=True)
    powers = [jnp.exp2((piece - peak) * to_base2) for piece in pieces]
    total = powers[0]
    weighted = powers[0] * grad_pieces[0]
    for power, grad_piece in zip(powers[1:], grad_pieces[1:]):
        total = total + power
        weighted = weighted + power * grad_piece
    inverse = 1.0 / jnp.sum(total, axis=0, keepdims=True)
    row_delta = jnp.sum(weighted, axis=0, keepdims=True) * inverse
    weights, score_grads = {}, {}
    for p in needed:
        weights[p] = (powers[p] * inverse).astype(jnp.bfloat16)
        score_grads[p] = (
            weights[p].astype(jnp.float32) * ((grad_pieces[p] - row_delta) * scale)
        ).astype(jnp.bfloat16)
    return query_heads, grad_heads, weights, score_grads


def dots(step, p, sums, key):
    query_heads, grad_heads, weights, score_grads = step
    parts = (
        jnp.dot(score_grads[p], query_heads, preferred_element_type=jnp.float32),
        jnp.dot(weights[p], grad_heads, preferred_element_type=jnp.float32),
    )
    sums[key] = parts if key not in sums else tuple(s + part for s, part in zip(sums[key], parts))


def query_part(strip_keys, score_grads):
    full = lax.dot_general(
        jnp.concatenate([score_grads[p] for p in range(REACH)], axis=0),
        strip_keys,
        (((0,), (0,)), ((), ())),
        preferred_element_type=jnp.float32,
    )
    lane = lax.broadcasted_iota(jnp.int32, (ROWS, HALF), 1)
    return jnp.where(lane < HEAD, full[:ROWS], full[ROWS:]).astype(jnp.bfloat16)


def block_of(ref, index):
    start = index * MESSAGE
    parts = [ref[start + i * ROWS : start + (i + 1) * ROWS, :] for i in range(4)]
    return (*parts, ref[start + 4 * ROWS : start + MESSAGE, :])


def write_sums(ref, sums, first):
    for block in range(2):
        for which in range(2):
            start = (2 * block + which) * ROWS
            ref[start : start + ROWS, :] = sums[first + block][which].astype(ref.dtype)


def read_sums(ref, first):
    return {
        first + block: tuple(
            ref[(2 * block + w) * ROWS : (2 * block + w + 1) * ROWS, :].astype(jnp.float32) for w in range(2)
        )
        for block in range(2)
    }


def own_kernel(core_ref, own_ref, behind_ref, far_ref, got_ref, keys, values, back_sums):
    every = slice(0, HALF)

    def place(mine, own):
        if mine == 0:
            near, next_, last = (behind_ref, own, 0), (got_ref.at[1], every, 2 * ROWS), (got_ref.at[1], every, 0)
        else:
            near, next_, last = (got_ref.at[0], every, 2 * ROWS), (behind_ref, own, 0), (far_ref, own, 0)
        for (ref, columns, start), first, count in ((last, 0, 1), (next_, 1, 2), (near, 3, 2)):
            for block in range(count):
                take(ref, start + block * 2 * ROWS, 1, columns, keys, first + block)
                take(ref, start + block * 2 * ROWS + ROWS, 1, columns, values, first + block)

    on_core(core_ref[0], place)
    blocks = [block_of(own_ref, block) for block in range(2)]
    for block in range(2):
        rows = slice((5 + block) * ROWS, (6 + block) * ROWS)
        keys[rows, :] = blocks[block][0]
        values[rows, :] = blocks[block][1]
    sums = {}
    for slot in range(2):
        strip_step(slot, 0, blocks[slot], keys, values, [1 - slot, 2 - slot], sums)
    write_sums(back_sums, sums, 1)


def strip_step(slot, first, block, keys, values, needed, sums):
    strip = slice((slot - first) * ROWS, (slot - first + REACH) * ROWS)
    step = query_step(keys[strip, :], values[strip, :], *block[2:], needed)
    for p in needed:
        if slot + p in (1, 2, 5, 6):
            dots(step, p, sums, slot + p)
    return step


def ahead_kernel(ahead_ref, keys7, values7, back_in, back_out, keys, values):
    for target, source, part in ((keys, keys7, 0), (values, values7, 1)):
        target[: 5 * ROWS, :] = source[2 * ROWS :, :]
        target[5 * ROWS :, :] = block_of(ahead_ref, 0)[part]
    sums = read_sums(back_in, 1)
    strip_step(2, 2, block_of(ahead_ref, 0), keys, values, [0], sums)
    write_sums(back_out, sums, 1)


def after_kernel(own_ref, ahead_ref, keys7, values7, query_grad, own_sums, keys, values):
    for target, source, part in ((keys, keys7, 0), (values, values7, 1)):
        target[: 7 * ROWS, :] = source[...]
        for block in range(2):
            target[(7 + block) * ROWS : (8 + block) * ROWS, :] = block_of(ahead_ref, block)[part]
    sums = {}
    for slot in range(4):
        block = block_of((own_ref, ahead_ref)[slot // 2], slot % 2)
        needed = list(range(REACH)) if slot < 2 else [5 - slot, 6 - slot]
        if slot < 2:
            strip = slice(slot * ROWS, (slot + REACH) * ROWS)
            step = query_step(keys[strip, :], values[strip, :], *block[2:], needed)
            for p in range(5 - slot, REACH):
                dots(step, p, sums, slot + p)
            query_grad[slot * ROWS : (slot + 1) * ROWS, :] = query_part(keys[strip, :], step[3])
        else:
            strip_step(slot, 0, block, keys, values, needed, sums)
    write_sums(own_sums, sums, 5)


def pick_kernel(core_ref, value_ref, out_ref):
    def place(mine, own):
        del own
        out_ref[...] = value_ref[:, (1 - mine) * HALF : (2 - mine) * HALF]

    on_core(core_ref[0], place)


def total_of(sums_ref, back_ref, block, which):
    rows = slice((2 * block + which) * ROWS, (2 * block + which + 1) * ROWS)
    return (sums_ref[rows, :] + back_ref[rows, :].astype(jnp.float32)).astype(jnp.bfloat16)


def swap_kernel(core_ref, query_grad, sums_ref, back_ref, out_ref):
    def place(mine, own):
        del own
        other = 1 - mine
        out_ref[:ROWS, :] = query_grad[other * ROWS : (other + 1) * ROWS, :]
        for which in range(2):
            out_ref[(1 + which) * ROWS : (2 + which) * ROWS, :] = total_of(sums_ref, back_ref, other, which)

    on_core(core_ref[0], place)


def last_kernel(core_ref, query_grad, sums_ref, back_ref, got_ref, out_q, out_k, out_v):
    def place(mine, own):
        other = slice((1 - mine) * HALF, (2 - mine) * HALF)
        out_q[:, own] = query_grad[mine * ROWS : (mine + 1) * ROWS, :]
        for which, out in ((0, out_k), (1, out_v)):
            out[:, own] = total_of(sums_ref, back_ref, mine, which)
        for at, out in enumerate((out_q, out_k, out_v)):
            out[:, other] = got_ref[1 - mine, at * ROWS : (at + 1) * ROWS, :]

    on_core(core_ref[0], place)


def call(kernel, name, outs, operands, scratch=(), work=0, scalar=True, grant=GRANT):
    outs = [jax.ShapeDtypeStruct(shape, dtype) for shape, dtype in outs]
    return pl.pallas_call(
        kernel,
        name=name,
        out_shape=outs,
        in_specs=[SMEM] * scalar + [VMEM] * (len(operands) - scalar),
        out_specs=[VMEM] * len(outs),
        scratch_shapes=[pltpu.VMEM((rows, HALF), jnp.bfloat16) for rows in scratch],
        cost_estimate=pl.CostEstimate(
            flops=work * 4 * 768 * 128 * 256, bytes_accessed=work * 1_000_000, transcendentals=work * 768 * 256
        ),
        compiler_params=pltpu.CompilerParams(vmem_limit_bytes=grant),
    )(*operands)


def on_device(queries, keys, values, out_grad, key_blocks):
    bf16, f32 = jnp.bfloat16, jnp.float32
    count = lax.axis_size("tm")
    core = lax.rem(lax.axis_index("tm"), 2)
    which = core.reshape(1)
    cores = [[2 * chip, 2 * chip + 1] for chip in range(count // 2)]

    def send(value, chips_from_core0, chips_from_core1):
        hops = (chips_from_core0, chips_from_core1)
        pairs = [(s, (s + 2 * hops[s % 2]) % count) for s in range(count) if hops[s % 2]]
        return lax.ppermute(value, "tm", pairs)

    def share(value):
        return lax.all_gather(value, "tm", axis_index_groups=cores)

    def half(value, other):
        return jnp.where((core == 0) != other, value[:, :HALF], value[:, HALF:])

    live = (key_blocks >= 0).astype(bf16)
    parts = [(x, i * ROWS, 0) for i, x in enumerate((keys, values, queries, out_grad))]
    parts += [(live, 4 * ROWS, 0), (live, 4 * ROWS, HALF)]
    own = placed(parts, MESSAGE, 2 * HALF)
    far = send(own[: 2 * ROWS], 0, 3)
    pair = share(own)
    behind = send(pair[:, : 2 * ROWS].reshape(4 * ROWS, 2 * HALF), 1, 2)
    ours = half(pair.reshape(2 * MESSAGE, 2 * HALF), False)
    ahead = send(ours, -1, -1)
    (far_half,) = call(pick_kernel, "pick", [((2 * ROWS, HALF), bf16)], (which, far), work=2)
    got = share(jnp.concatenate([far_half, half(behind, True)], axis=0))
    seven, sums_of = ((7 * ROWS, HALF), bf16), (4 * ROWS, HALF)
    keys7, values7, back = call(
        own_kernel, "own", [seven, seven, (sums_of, f32)], (which, ours, behind, far, got), work=2
    )
    (back,) = call(
        ahead_kernel, "ahead", [(sums_of, bf16)], (ahead, keys7, values7, back),
        (6 * ROWS, 6 * ROWS), work=1, scalar=False,
    )
    returned = send(back, -2, -2)
    query_grad, sums = call(
        after_kernel, "after", [((2 * ROWS, HALF), bf16), (sums_of, f32)], (ours, ahead, keys7, values7),
        (9 * ROWS, 9 * ROWS), work=4, scalar=False,
    )
    (swap,) = call(
        swap_kernel, "swap", [((3 * ROWS, HALF), bf16)], (which, query_grad, sums, returned)
    )
    return tuple(
        call(
            last_kernel, "last", [((ROWS, 2 * HALF), bf16)] * 3,
            (which, query_grad, sums, returned, share(swap)),
        )
    )


def solution(mesh):
    rows = P(("groups", "tm"), None)
    return jax.shard_map(
        on_device,
        mesh=mesh,
        in_specs=(rows,) * 5,
        out_specs=(rows,) * 3,
        check_vma=False,
    )
```

```python
import math

import jax
import jax.numpy as jnp
from jax import lax
from jax.experimental import pallas as pl
from jax.experimental.pallas import tpu as pltpu
from jax.sharding import PartitionSpec as P

HEAD = 64
ROWS = 128
HALF = 128
REACH = 6
FLAGS = 16
MESSAGE = 4 * ROWS + FLAGS
MASKED = -1e30
GRANT = 16 * 1024 * 1024

VMEM = pl.BlockSpec(memory_space=pltpu.VMEM)
SMEM = pl.BlockSpec(memory_space=pltpu.SMEM)


def placed(parts, rows, columns):
    total = None
    for part, row, column in parts:
        space = [(row, rows - row - part.shape[0], 0), (column, columns - column - part.shape[1], 0)]
        padded = lax.pad(part, jnp.array(-jnp.inf, part.dtype), space)
        total = padded if total is None else jnp.maximum(total, padded)
    return total


def by_head(rows):
    lane = lax.broadcasted_iota(jnp.int32, rows.shape, 1)
    zero = jnp.zeros_like(rows)
    return jnp.concatenate(
        [jnp.where(lane < HEAD, rows, zero), jnp.where(lane >= HEAD, rows, zero)], axis=0
    )


def take(source, start, count, columns, target, at):
    target[at * ROWS : (at + count) * ROWS, :] = source[start : start + count * ROWS, columns]


def on_core(core, place):
    own = (slice(0, HALF), slice(HALF, 2 * HALF))
    for mine in range(2):

        @pl.when(core == mine)
        def _(mine=mine):
            place(mine, own[mine])


def live_at(live, distance):
    return jnp.broadcast_to(live[:1, distance : distance + 1], (1, 2 * ROWS)) > 0.0


def query_step(strip_keys, strip_values, query_rows, grad_rows, live, needed):
    scale = 1.0 / math.sqrt(HEAD)
    to_base2 = scale * math.log2(math.e)
    both = (((1,), (1,)), ((), ()))
    key_row = lax.broadcasted_iota(jnp.int32, (ROWS, 2 * ROWS), 0)
    query_row = lax.broadcasted_iota(jnp.int32, (ROWS, 2 * ROWS), 1) & (ROWS - 1)
    query_heads = by_head(query_rows)
    grad_heads = by_head(grad_rows)
    live = live.astype(jnp.float32)
    scores = lax.dot_general(strip_keys, query_heads, both, preferred_element_type=jnp.float32)
    prob_grad = lax.dot_general(
        strip_values, grad_heads, both, preferred_element_type=jnp.float32
    )
    pieces = [scores[p * ROWS : (p + 1) * ROWS] for p in range(REACH)]
    pieces[0] = jnp.where(live_at(live, 5), pieces[0], MASKED)
    pieces[1] = jnp.where(live_at(live, 4), pieces[1], MASKED)
    pieces[5] = jnp.where(key_row <= query_row, pieces[5], MASKED)
    grad_pieces = [prob_grad[p * ROWS : (p + 1) * ROWS] for p in range(REACH)]
    peak = pieces[0]
    for piece in pieces[1:]:
        peak = jnp.maximum(peak, piece)
    peak = jnp.max(peak, axis=0, keepdims=True)
    powers = [jnp.exp2((piece - peak) * to_base2) for piece in pieces]
    total = powers[0]
    weighted = powers[0] * grad_pieces[0]
    for power, grad_piece in zip(powers[1:], grad_pieces[1:]):
        total = total + power
        weighted = weighted + power * grad_piece
    inverse = 1.0 / jnp.sum(total, axis=0, keepdims=True)
    row_delta = jnp.sum(weighted, axis=0, keepdims=True) * inverse
    weights, score_grads = {}, {}
    for p in needed:
        weights[p] = (powers[p] * inverse).astype(jnp.bfloat16)
        score_grads[p] = (
            weights[p].astype(jnp.float32) * ((grad_pieces[p] - row_delta) * scale)
        ).astype(jnp.bfloat16)
    return query_heads, grad_heads, weights, score_grads


def dots(step, p, sums, key):
    query_heads, grad_heads, weights, score_grads = step
    parts = (
        jnp.dot(score_grads[p], query_heads, preferred_element_type=jnp.float32),
        jnp.dot(weights[p], grad_heads, preferred_element_type=jnp.float32),
    )
    sums[key] = parts if key not in sums else tuple(s + part for s, part in zip(sums[key], parts))


def query_part(strip_keys, score_grads):
    full = lax.dot_general(
        jnp.concatenate([score_grads[p] for p in range(REACH)], axis=0),
        strip_keys,
        (((0,), (0,)), ((), ())),
        preferred_element_type=jnp.float32,
    )
    lane = lax.broadcasted_iota(jnp.int32, (ROWS, HALF), 1)
    return jnp.where(lane < HEAD, full[:ROWS], full[ROWS:]).astype(jnp.bfloat16)


def block_of(ref, index):
    start = index * MESSAGE
    parts = [ref[start + i * ROWS : start + (i + 1) * ROWS, :] for i in range(4)]
    return (*parts, ref[start + 4 * ROWS : start + MESSAGE, :])


def write_sums(ref, sums, first):
    for block in range(2):
        for which in range(2):
            start = (2 * block + which) * ROWS
            ref[start : start + ROWS, :] = sums[first + block][which].astype(ref.dtype)


def read_sums(ref, first):
    return {
        first + block: tuple(
            ref[(2 * block + w) * ROWS : (2 * block + w + 1) * ROWS, :].astype(jnp.float32) for w in range(2)
        )
        for block in range(2)
    }


def own_kernel(core_ref, own_ref, behind_ref, far_ref, got_ref, keys, values, back_sums):
    every = slice(0, HALF)

    def place(mine, own):
        if mine == 0:
            near, next_, last = (got_ref.at[1], every, 2 * ROWS), (behind_ref, own, 0), (got_ref.at[1], every, 0)
        else:
            near, next_, last = (behind_ref, own, 0), (got_ref.at[0], every, 2 * ROWS), (far_ref, own, 0)
        for (ref, columns, start), first, count in ((last, 0, 1), (next_, 1, 2), (near, 3, 2)):
            for block in range(count):
                take(ref, start + block * 2 * ROWS, 1, columns, keys, first + block)
                take(ref, start + block * 2 * ROWS + ROWS, 1, columns, values, first + block)

    on_core(core_ref[0], place)
    blocks = [block_of(own_ref, block) for block in range(2)]
    for block in range(2):
        rows = slice((5 + block) * ROWS, (6 + block) * ROWS)
        keys[rows, :] = blocks[block][0]
        values[rows, :] = blocks[block][1]
    sums = {}
    for slot in range(2):
        strip_step(slot, 0, blocks[slot], keys, values, [1 - slot, 2 - slot], sums)
    write_sums(back_sums, sums, 1)


def strip_step(slot, first, block, keys, values, needed, sums):
    strip = slice((slot - first) * ROWS, (slot - first + REACH) * ROWS)
    step = query_step(keys[strip, :], values[strip, :], *block[2:], needed)
    for p in needed:
        if slot + p in (1, 2, 5, 6):
            dots(step, p, sums, slot + p)
    return step


def ahead_kernel(ahead_ref, keys7, values7, back_in, back_out, keys, values):
    for target, source, part in ((keys, keys7, 0), (values, values7, 1)):
        target[: 5 * ROWS, :] = source[2 * ROWS :, :]
        target[5 * ROWS :, :] = block_of(ahead_ref, 0)[part]
    sums = read_sums(back_in, 1)
    strip_step(2, 2, block_of(ahead_ref, 0), keys, values, [0], sums)
    write_sums(back_out, sums, 1)


def after_kernel(own_ref, ahead_ref, keys7, values7, query_grad, own_sums, keys, values):
    for target, source, part in ((keys, keys7, 0), (values, values7, 1)):
        target[: 7 * ROWS, :] = source[...]
        for block in range(2):
            target[(7 + block) * ROWS : (8 + block) * ROWS, :] = block_of(ahead_ref, block)[part]
    sums = {}
    for slot in range(4):
        block = block_of((own_ref, ahead_ref)[slot // 2], slot % 2)
        needed = list(range(REACH)) if slot < 2 else [5 - slot, 6 - slot]
        if slot < 2:
            strip = slice(slot * ROWS, (slot + REACH) * ROWS)
            step = query_step(keys[strip, :], values[strip, :], *block[2:], needed)
            for p in range(5 - slot, REACH):
                dots(step, p, sums, slot + p)
            query_grad[slot * ROWS : (slot + 1) * ROWS, :] = query_part(keys[strip, :], step[3])
        else:
            strip_step(slot, 0, block, keys, values, needed, sums)
    write_sums(own_sums, sums, 5)


def pick_kernel(core_ref, value_ref, out_ref):
    def place(mine, own):
        del own
        out_ref[...] = value_ref[:, (1 - mine) * HALF : (2 - mine) * HALF]

    on_core(core_ref[0], place)


def total_of(sums_ref, back_ref, block, which):
    rows = slice((2 * block + which) * ROWS, (2 * block + which + 1) * ROWS)
    return (sums_ref[rows, :] + back_ref[rows, :].astype(jnp.float32)).astype(jnp.bfloat16)


def swap_kernel(core_ref, query_grad, sums_ref, back_ref, out_ref):
    def place(mine, own):
        del own
        other = 1 - mine
        out_ref[:ROWS, :] = query_grad[other * ROWS : (other + 1) * ROWS, :]
        for which in range(2):
            out_ref[(1 + which) * ROWS : (2 + which) * ROWS, :] = total_of(sums_ref, back_ref, other, which)

    on_core(core_ref[0], place)


def last_kernel(core_ref, query_grad, sums_ref, back_ref, got_ref, out_q, out_k, out_v):
    def place(mine, own):
        other = slice((1 - mine) * HALF, (2 - mine) * HALF)
        out_q[:, own] = query_grad[mine * ROWS : (mine + 1) * ROWS, :]
        for which, out in ((0, out_k), (1, out_v)):
            out[:, own] = total_of(sums_ref, back_ref, mine, which)
        for at, out in enumerate((out_q, out_k, out_v)):
            out[:, other] = got_ref[1 - mine, at * ROWS : (at + 1) * ROWS, :]

    on_core(core_ref[0], place)


def call(kernel, name, outs, operands, scratch=(), work=0, scalar=True, grant=GRANT):
    outs = [jax.ShapeDtypeStruct(shape, dtype) for shape, dtype in outs]
    return pl.pallas_call(
        kernel,
        name=name,
        out_shape=outs,
        in_specs=[SMEM] * scalar + [VMEM] * (len(operands) - scalar),
        out_specs=[VMEM] * len(outs),
        scratch_shapes=[pltpu.VMEM((rows, HALF), jnp.bfloat16) for rows in scratch],
        cost_estimate=pl.CostEstimate(
            flops=work * 4 * 768 * 128 * 256, bytes_accessed=work * 1_000_000, transcendentals=work * 768 * 256
        ),
        compiler_params=pltpu.CompilerParams(vmem_limit_bytes=grant),
    )(*operands)


def on_device(queries, keys, values, out_grad, key_blocks):
    bf16, f32 = jnp.bfloat16, jnp.float32
    count = lax.axis_size("tm")
    core = lax.rem(lax.axis_index("tm"), 2)
    which = core.reshape(1)
    cores = [[2 * chip, 2 * chip + 1] for chip in range(count // 2)]

    def send(value, chips_from_core0, chips_from_core1):
        hops = (chips_from_core0, chips_from_core1)
        pairs = [(s, (s + 2 * hops[s % 2]) % count) for s in range(count) if hops[s % 2]]
        return lax.ppermute(value, "tm", pairs)

    def share(value):
        return lax.all_gather(value, "tm", axis_index_groups=cores)

    def half(value, other):
        return jnp.where((core == 0) != other, value[:, :HALF], value[:, HALF:])

    live = (key_blocks >= 0).astype(bf16)
    parts = [(x, i * ROWS, 0) for i, x in enumerate((keys, values, queries, out_grad))]
    parts += [(live, 4 * ROWS, 0), (live, 4 * ROWS, HALF)]
    own = placed(parts, MESSAGE, 2 * HALF)
    far = send(own[: 2 * ROWS], 0, 3)
    pair = share(own)
    behind = send(pair[:, : 2 * ROWS].reshape(4 * ROWS, 2 * HALF), 2, 1)
    ours = half(pair.reshape(2 * MESSAGE, 2 * HALF), False)
    ahead = send(ours, -1, -1)
    (far_half,) = call(pick_kernel, "pick", [((2 * ROWS, HALF), bf16)], (which, far), work=2)
    got = share(jnp.concatenate([far_half, half(behind, True)], axis=0))
    seven, sums_of = ((7 * ROWS, HALF), bf16), (4 * ROWS, HALF)
    keys7, values7, back = call(
        own_kernel, "own", [seven, seven, (sums_of, f32)], (which, ours, behind, far, got), work=2
    )
    (back,) = call(
        ahead_kernel, "ahead", [(sums_of, bf16)], (ahead, keys7, values7, back),
        (6 * ROWS, 6 * ROWS), work=1, scalar=False,
    )
    returned = send(back, -2, -2)
    query_grad, sums = call(
        after_kernel, "after", [((2 * ROWS, HALF), bf16), (sums_of, f32)], (ours, ahead, keys7, values7),
        (9 * ROWS, 9 * ROWS), work=4, scalar=False,
    )
    (swap,) = call(
        swap_kernel, "swap", [((3 * ROWS, HALF), bf16)], (which, query_grad, sums, returned)
    )
    return tuple(
        call(
            last_kernel, "last", [((ROWS, 2 * HALF), bf16)] * 3,
            (which, query_grad, sums, returned, share(swap)),
        )
    )


def solution(mesh):
    rows = P(("groups", "tm"), None)
    return jax.shard_map(
        on_device,
        mesh=mesh,
        in_specs=(rows,) * 5,
        out_specs=(rows,) * 3,
        check_vma=False,
    )
```

```python
import math

import jax
import jax.numpy as jnp
from jax import lax
from jax.experimental import pallas as pl
from jax.experimental.pallas import tpu as pltpu
from jax.sharding import PartitionSpec as P

HEAD = 64
ROWS = 128
HALF = 128
REACH = 6
FLAGS = 16
MESSAGE = 4 * ROWS + FLAGS
MASKED = -1e30
GRANT = 16 * 1024 * 1024

VMEM = pl.BlockSpec(memory_space=pltpu.VMEM)
SMEM = pl.BlockSpec(memory_space=pltpu.SMEM)


def placed(parts, rows, columns):
    total = None
    for part, row, column in parts:
        space = [(row, rows - row - part.shape[0], 0), (column, columns - column - part.shape[1], 0)]
        padded = lax.pad(part, jnp.array(-jnp.inf, part.dtype), space)
        total = padded if total is None else jnp.maximum(total, padded)
    return total


def by_head(rows):
    lane = lax.broadcasted_iota(jnp.int32, rows.shape, 1)
    zero = jnp.zeros_like(rows)
    return jnp.concatenate(
        [jnp.where(lane < HEAD, rows, zero), jnp.where(lane >= HEAD, rows, zero)], axis=0
    )


def take(source, start, count, columns, target, at):
    target[at * ROWS : (at + count) * ROWS, :] = source[start : start + count * ROWS, columns]


def on_core(core, place):
    own = (slice(0, HALF), slice(HALF, 2 * HALF))
    for mine in range(2):

        @pl.when(core == mine)
        def _(mine=mine):
            place(mine, own[mine])


def live_at(live, distance):
    return jnp.broadcast_to(live[:1, distance : distance + 1], (1, 2 * ROWS)) > 0.0


def query_step(strip_keys, strip_values, query_rows, grad_rows, live, needed):
    scale = 1.0 / math.sqrt(HEAD)
    to_base2 = scale * math.log2(math.e)
    both = (((1,), (1,)), ((), ()))
    key_row = lax.broadcasted_iota(jnp.int32, (ROWS, 2 * ROWS), 0)
    query_row = lax.broadcasted_iota(jnp.int32, (ROWS, 2 * ROWS), 1) & (ROWS - 1)
    query_heads = by_head(query_rows)
    grad_heads = by_head(grad_rows)
    live = live.astype(jnp.float32)
    scores = lax.dot_general(strip_keys, query_heads, both, preferred_element_type=jnp.float32)
    prob_grad = lax.dot_general(
        strip_values, grad_heads, both, preferred_element_type=jnp.float32
    )
    pieces = [scores[p * ROWS : (p + 1) * ROWS] for p in range(REACH)]
    pieces[0] = jnp.where(live_at(live, 5), pieces[0], MASKED)
    pieces[1] = jnp.where(live_at(live, 4), pieces[1], MASKED)
    pieces[5] = jnp.where(key_row <= query_row, pieces[5], MASKED)
    grad_pieces = [prob_grad[p * ROWS : (p + 1) * ROWS] for p in range(REACH)]
    peak = pieces[0]
    for piece in pieces[1:]:
        peak = jnp.maximum(peak, piece)
    peak = jnp.max(peak, axis=0, keepdims=True)
    powers = [jnp.exp2((piece - peak) * to_base2) for piece in pieces]
    total = powers[0]
    weighted = powers[0] * grad_pieces[0]
    for power, grad_piece in zip(powers[1:], grad_pieces[1:]):
        total = total + power
        weighted = weighted + power * grad_piece
    inverse = 1.0 / jnp.sum(total, axis=0, keepdims=True)
    row_delta = jnp.sum(weighted, axis=0, keepdims=True) * inverse
    weights, score_grads = {}, {}
    for p in needed:
        weights[p] = (powers[p] * inverse).astype(jnp.bfloat16)
        score_grads[p] = (
            weights[p].astype(jnp.float32) * ((grad_pieces[p] - row_delta) * scale)
        ).astype(jnp.bfloat16)
    return query_heads, grad_heads, weights, score_grads


def dots(step, p, sums, key):
    query_heads, grad_heads, weights, score_grads = step
    parts = (
        jnp.dot(score_grads[p], query_heads, preferred_element_type=jnp.float32),
        jnp.dot(weights[p], grad_heads, preferred_element_type=jnp.float32),
    )
    sums[key] = parts if key not in sums else tuple(s + part for s, part in zip(sums[key], parts))


def query_part(strip_keys, score_grads):
    full = lax.dot_general(
        jnp.concatenate([score_grads[p] for p in range(REACH)], axis=0),
        strip_keys,
        (((0,), (0,)), ((), ())),
        preferred_element_type=jnp.float32,
    )
    lane = lax.broadcasted_iota(jnp.int32, (ROWS, HALF), 1)
    return jnp.where(lane < HEAD, full[:ROWS], full[ROWS:]).astype(jnp.bfloat16)


def block_of(ref, index):
    start = index * MESSAGE
    parts = [ref[start + i * ROWS : start + (i + 1) * ROWS, :] for i in range(4)]
    return (*parts, ref[start + 4 * ROWS : start + MESSAGE, :])


def write_sums(ref, sums, first):
    for block in range(2):
        for which in range(2):
            start = (2 * block + which) * ROWS
            ref[start : start + ROWS, :] = sums[first + block][which].astype(ref.dtype)


def read_sums(ref, first):
    return {
        first + block: tuple(
            ref[(2 * block + w) * ROWS : (2 * block + w + 1) * ROWS, :].astype(jnp.float32) for w in range(2)
        )
        for block in range(2)
    }


def own_kernel(core_ref, own_ref, behind_ref, far_ref, got_ref, keys, values, back_sums):
    every = slice(0, HALF)

    def place(mine, own):
        if mine == 0:
            near, next_, last = (got_ref.at[1], every, 2 * ROWS), (behind_ref, own, 0), (got_ref.at[1], every, 0)
        else:
            near, next_, last = (behind_ref, own, 0), (got_ref.at[0], every, 2 * ROWS), (far_ref, own, 0)
        for (ref, columns, start), first, count in ((last, 0, 1), (next_, 1, 2), (near, 3, 2)):
            for block in range(count):
                take(ref, start + block * 2 * ROWS, 1, columns, keys, first + block)
                take(ref, start + block * 2 * ROWS + ROWS, 1, columns, values, first + block)

    on_core(core_ref[0], place)
    blocks = [block_of(own_ref, block) for block in range(2)]
    for block in range(2):
        rows = slice((5 + block) * ROWS, (6 + block) * ROWS)
        keys[rows, :] = blocks[block][0]
        values[rows, :] = blocks[block][1]
    sums = {}
    for slot in range(2):
        strip_step(slot, 0, blocks[slot], keys, values, [1 - slot, 2 - slot], sums)
    write_sums(back_sums, sums, 1)


def strip_step(slot, first, block, keys, values, needed, sums):
    strip = slice((slot - first) * ROWS, (slot - first + REACH) * ROWS)
    step = query_step(keys[strip, :], values[strip, :], *block[2:], needed)
    for p in needed:
        if slot + p in (1, 2, 5, 6):
            dots(step, p, sums, slot + p)
    return step


def ahead_kernel(ahead_ref, keys7, values7, back_in, back_out):
    block = block_of(ahead_ref, 0)
    strips = [
        jnp.concatenate([ref[2 * ROWS :, :], block[part]], axis=0)
        for part, ref in enumerate((keys7, values7))
    ]
    sums = read_sums(back_in, 1)
    dots(query_step(*strips, *block[2:], [0]), 0, sums, 2)
    write_sums(back_out, sums, 1)


def after_kernel(own_ref, ahead_ref, keys7, values7, query_grad, own_sums, keys, values):
    for target, source, part in ((keys, keys7, 0), (values, values7, 1)):
        target[: 7 * ROWS, :] = source[...]
        for block in range(2):
            target[(7 + block) * ROWS : (8 + block) * ROWS, :] = block_of(ahead_ref, block)[part]
    sums = {}
    for slot in range(4):
        block = block_of((own_ref, ahead_ref)[slot // 2], slot % 2)
        needed = list(range(REACH)) if slot < 2 else [5 - slot, 6 - slot]
        if slot < 2:
            strip = slice(slot * ROWS, (slot + REACH) * ROWS)
            step = query_step(keys[strip, :], values[strip, :], *block[2:], needed)
            for p in range(5 - slot, REACH):
                dots(step, p, sums, slot + p)
            query_grad[slot * ROWS : (slot + 1) * ROWS, :] = query_part(keys[strip, :], step[3])
        else:
            strip_step(slot, 0, block, keys, values, needed, sums)
    write_sums(own_sums, sums, 5)


def pick_kernel(core_ref, value_ref, out_ref):
    def place(mine, own):
        del own
        out_ref[...] = value_ref[:, (1 - mine) * HALF : (2 - mine) * HALF]

    on_core(core_ref[0], place)


def total_of(sums_ref, back_ref, block, which):
    rows = slice((2 * block + which) * ROWS, (2 * block + which + 1) * ROWS)
    return (sums_ref[rows, :] + back_ref[rows, :].astype(jnp.float32)).astype(jnp.bfloat16)


def swap_kernel(core_ref, query_grad, sums_ref, back_ref, out_ref):
    def place(mine, own):
        del own
        other = 1 - mine
        out_ref[:ROWS, :] = query_grad[other * ROWS : (other + 1) * ROWS, :]
        for which in range(2):
            out_ref[(1 + which) * ROWS : (2 + which) * ROWS, :] = total_of(sums_ref, back_ref, other, which)

    on_core(core_ref[0], place)


def last_kernel(core_ref, query_grad, sums_ref, back_ref, got_ref, out_q, out_k, out_v):
    def place(mine, own):
        other = slice((1 - mine) * HALF, (2 - mine) * HALF)
        out_q[:, own] = query_grad[mine * ROWS : (mine + 1) * ROWS, :]
        for which, out in ((0, out_k), (1, out_v)):
            out[:, own] = total_of(sums_ref, back_ref, mine, which)
        for at, out in enumerate((out_q, out_k, out_v)):
            out[:, other] = got_ref[1 - mine, at * ROWS : (at + 1) * ROWS, :]

    on_core(core_ref[0], place)


def call(kernel, name, outs, operands, scratch=(), work=0, scalar=True, grant=GRANT):
    outs = [jax.ShapeDtypeStruct(shape, dtype) for shape, dtype in outs]
    return pl.pallas_call(
        kernel,
        name=name,
        out_shape=outs,
        in_specs=[SMEM] * scalar + [VMEM] * (len(operands) - scalar),
        out_specs=[VMEM] * len(outs),
        scratch_shapes=[pltpu.VMEM((rows, HALF), jnp.bfloat16) for rows in scratch],
        cost_estimate=pl.CostEstimate(
            flops=work * 4 * 768 * 128 * 256, bytes_accessed=work * 1_000_000, transcendentals=work * 768 * 256
        ),
        compiler_params=pltpu.CompilerParams(vmem_limit_bytes=grant),
    )(*operands)


def on_device(queries, keys, values, out_grad, key_blocks):
    bf16, f32 = jnp.bfloat16, jnp.float32
    count = lax.axis_size("tm")
    core = lax.rem(lax.axis_index("tm"), 2)
    which = core.reshape(1)
    cores = [[2 * chip, 2 * chip + 1] for chip in range(count // 2)]

    def send(value, chips_from_core0, chips_from_core1):
        hops = (chips_from_core0, chips_from_core1)
        pairs = [(s, (s + 2 * hops[s % 2]) % count) for s in range(count) if hops[s % 2]]
        return lax.ppermute(value, "tm", pairs)

    def share(value):
        return lax.all_gather(value, "tm", axis_index_groups=cores)

    def half(value, other):
        return jnp.where((core == 0) != other, value[:, :HALF], value[:, HALF:])

    live = (key_blocks >= 0).astype(bf16)
    parts = [(x, i * ROWS, 0) for i, x in enumerate((keys, values, queries, out_grad))]
    parts += [(live, 4 * ROWS, 0), (live, 4 * ROWS, HALF)]
    own = placed(parts, MESSAGE, 2 * HALF)
    far = send(own[: 2 * ROWS], 0, 3)
    pair = share(own)
    behind = send(pair[:, : 2 * ROWS].reshape(4 * ROWS, 2 * HALF), 2, 1)
    ours = half(pair.reshape(2 * MESSAGE, 2 * HALF), False)
    ahead = send(ours, -1, -1)
    (far_half,) = call(pick_kernel, "pick", [((2 * ROWS, HALF), bf16)], (which, far), work=2)
    got = share(jnp.concatenate([far_half, half(behind, True)], axis=0))
    seven, sums_of = ((7 * ROWS, HALF), bf16), (4 * ROWS, HALF)
    keys7, values7, back = call(
        own_kernel, "own", [seven, seven, (sums_of, f32)], (which, ours, behind, far, got), work=2
    )
    (back,) = call(
        ahead_kernel, "ahead", [(sums_of, bf16)], (ahead, keys7, values7, back),
        work=1, scalar=False,
    )
    returned = send(back, -2, -2)
    query_grad, sums = call(
        after_kernel, "after", [((2 * ROWS, HALF), bf16), (sums_of, f32)], (ours, ahead, keys7, values7),
        (9 * ROWS, 9 * ROWS), work=4, scalar=False,
    )
    (swap,) = call(
        swap_kernel, "swap", [((3 * ROWS, HALF), bf16)], (which, query_grad, sums, returned)
    )
    return tuple(
        call(
            last_kernel, "last", [((ROWS, 2 * HALF), bf16)] * 3,
            (which, query_grad, sums, returned, share(swap)),
        )
    )


def solution(mesh):
    rows = P(("groups", "tm"), None)
    return jax.shard_map(
        on_device,
        mesh=mesh,
        in_specs=(rows,) * 5,
        out_specs=(rows,) * 3,
        check_vma=False,
    )
```
